32 devices in a mesh: layer: 4 (over x, core), latent: 4 (over z), row: 2 (over y).
Axes of the slice: x: 2, y: 2, z: 4, core: 2. Of those that a mesh axis runs over, the one named last changes fastest.
Arguments:
- inputs: bfloat16 [1024, 4, 3584], P('row', 'layer'), may hold values from -6 to 6
- clean_acts: bfloat16 [1024, 4, 3584], P('row', 'layer'), may hold values from -6 to 6
- enc_weight: bfloat16 [4, 3584, 12288], P('layer', None, 'latent'), may hold values from -0.0625 to 0.0625
- enc_bias: float32 [12288], P('latent'), may hold values from -3 to 3
- dec_weight: bfloat16 [4, 12288, 3584], P('layer', 'latent'), may hold values from -0.109375 to 0.109375
- dec_bias: float32 [4, 3584], P('layer'), may hold values from -3 to 3
- pairing: int32 [1024], replicated, may hold values from 0 to 1023, each once
- targets: int32 [1024], replicated, may hold values from 0 to 12287
Outputs:
- input_grad: bfloat16 [1024, 4, 3584], P('row', 'layer', 'latent')
The draws below stay inside these ranges and needn't reach their ends.
Inputs may be any that keep to these rules, and one draw needn't show every extreme that they name: pairing is a permutation of the rows.
All inputs are finite; a program needn't handle non-finite values.
Results may differ from the reference program's by a relative error of at most 0.018.
Values may be sent and summed in bfloat16 or wider, within the bound.
No kernel may reach another device: no remote copies, remote signals or barrier semaphores. Data moves between devices by JAX's collectives and lax.ppermute only.
A program may use at most 128 MiB of HBM per device.

```python
import jax
import jax.numpy as jnp

D = 3584
LATENTS = 12288
LAYERS = 4
ROWS = 1024
N_LATENT = 4


def touch_ends(result, key, low, high):
    longest = result.shape.index(max(result.shape))
    spots = []
    for shift in (0, 1):
        where = [jax.random.randint(jax.random.fold_in(key, axis), (), 0, length) for axis, length in enumerate(result.shape)]
        where[longest] = (where[longest] + shift) % result.shape[longest]
        spots.append(tuple(where))
    return result.at[spots[0]].set(low).at[spots[1]].set(high)


def raised(array, key, source, target, shards_of, factor):
    owner, partner = [(jnp.arange(array.shape[axis_at]) // (array.shape[axis_at] // shards_of)).reshape([-1 if axis == axis_at else 1 for axis in range(array.ndim)]) for axis_at in (source, target)]
    chosen = jax.random.permutation(key, shards_of)[partner]
    strong = (owner == chosen) | (owner == (partner + shards_of // 2) % shards_of)
    return jnp.where(strong, factor * array, array)


def block_levels(key, shape, cuts, least, high):
    level, own = 1.0, jax.random.fold_in(key, 6)
    for position, parts in cuts:
        draws = jnp.exp(jax.random.uniform(jax.random.fold_in(own, position), (parts,), jnp.float32, least / len(cuts), high / len(cuts)))
        level = level * jnp.repeat(draws, shape[position] // parts).reshape([-1 if axis == position else 1 for axis in range(len(shape))])
    return level


def normal_values(stream_key, extent, width, reach, cuts=(), kind=jnp.bfloat16):
    entries = width * jax.random.normal(stream_key, extent, jnp.float32)
    if cuts:
        entries = entries * block_levels(stream_key, extent, cuts, -0.22, 0.18)
    return jnp.clip(entries, -reach, reach).astype(kind)


def noise_with(stream_key, shape, scale, most, cuts, heavy, held_as=jnp.bfloat16):
    array = scale * jax.random.normal(stream_key, shape, jnp.float32)
    if cuts:
        array = array * block_levels(stream_key, shape, cuts, -0.22, 0.18)
    return jnp.clip(raised(array, jax.random.fold_in(stream_key, 3), *heavy), -most, most).astype(held_as)


def setup_inputs(seed: int = 0) -> dict:
    key_of = jax.random.split(jax.random.key(seed), 9)
    inputs = normal_values(key_of[0], (ROWS, LAYERS, D), 1.0, 6.0, ((0, 2), (1, 4)))
    clean_acts = normal_values(key_of[1], (ROWS, LAYERS, D), 1.0, 6.0, ((0, 2), (1, 4)))
    enc_weight = noise_with(key_of[2], (LAYERS, D, LATENTS), (D * LAYERS) ** -0.5, 0.0625, ((0, 4), (2, 4)), (2, 1, 4, 2.0))
    enc_bias = normal_values(key_of[3], (LATENTS,), 0.5, 3.0, ((0, 4),), jnp.float32)
    dec_weight = normal_values(key_of[4], (LAYERS, LATENTS, D), (LATENTS // 4) ** -0.5, 0.109375, ((0, 4), (1, 4)))
    dec_bias = normal_values(key_of[5], (LAYERS, D), 0.5, 3.0, ((0, 4),), jnp.float32)
    pairing = jax.random.permutation(key_of[6], ROWS).astype(jnp.int32)
    targets = touch_ends(jax.random.randint(key_of[7], (ROWS,), 0, LATENTS), jax.random.fold_in(key_of[7], 1), 0, LATENTS - 1).astype(jnp.int32)
    return {"inputs": inputs, "clean_acts": clean_acts, "enc_weight": enc_weight, "enc_bias": enc_bias, "dec_weight": dec_weight, "dec_bias": dec_bias, "pairing": pairing, "targets": targets}


MARGIN = 16.0


def reference(inputs, clean_acts, enc_weight, enc_bias, dec_weight, dec_bias, pairing, targets):
    group = LATENTS // N_LATENT
    preact = jnp.zeros((ROWS, LATENTS), jnp.float32)
    for layer_idx in range(LAYERS):
        preact = preact + jnp.dot(inputs[:, layer_idx], enc_weight[layer_idx], preferred_element_type=jnp.float32)
    preact = preact + enc_bias
    features = jnp.maximum(preact, 0.0).astype(jnp.bfloat16)
    feat_split = features.reshape(ROWS, N_LATENT, group)
    feat_grad = jnp.zeros((ROWS, LATENTS), jnp.float32)
    for layer_idx in range(LAYERS):
        dec_split = dec_weight[layer_idx].reshape(N_LATENT, group, D)
        partials = jnp.einsum("rng,ngd->nrd", feat_split, dec_split, preferred_element_type=jnp.float32)
        recon = jnp.sum(partials.astype(jnp.bfloat16).astype(jnp.float32), axis=0) + dec_bias[layer_idx]
        recon_error = (recon - clean_acts[:, layer_idx].astype(jnp.float32)).astype(jnp.bfloat16)
        layer_term = jnp.dot(recon_error, dec_weight[layer_idx].T, preferred_element_type=jnp.float32)
        feat_grad = feat_grad + layer_term.astype(jnp.bfloat16).astype(jnp.float32)
    latent_ids = jnp.arange(LATENTS, dtype=jnp.int32)
    target_hot = (targets[:, None] == latent_ids[None, :]).astype(jnp.float32)
    moved = jnp.zeros((ROWS, LATENTS), jnp.float32).at[pairing].add(target_hot)
    margin_table = target_hot - moved
    pre_grad = jnp.where(preact > 0, feat_grad - MARGIN * margin_table, 0.0).astype(jnp.bfloat16)
    pre_split = pre_grad.reshape(ROWS, N_LATENT, group)
    outputs = []
    for layer_idx in range(LAYERS):
        enc_split = enc_weight[layer_idx].reshape(D, N_LATENT, group)
        partials = jnp.einsum("rng,dng->nrd", pre_split, enc_split, preferred_element_type=jnp.float32)
        total = jnp.sum(partials.astype(jnp.bfloat16).astype(jnp.float32), axis=0)
        outputs.append(total.astype(jnp.bfloat16))
    return jnp.stack(outputs, axis=1)
```

```python
import jax
import jax.numpy as jnp
from jax import lax
from jax.experimental import pallas as pl
from jax.experimental.pallas import tpu as pltpu
from jax.sharding import PartitionSpec as P

MARGIN = 16.0
CHUNKS = (128, 128, 128, 128)
ORDER = (
    ("A", 0), ("A", 1), ("A2", 0), ("A", 2), ("A2", 1), ("A", 3), ("A2", 2), ("A3", 0), ("A2", 3), ("B", 0), ("A3", 1), ("B", 1), ("A3", 2), ("S2", 0), ("B", 2), ("A3", 3), ("S2", 1), ("B", 3), ("S3", 0),
    ("S2", 2), ("S3", 1), ("C", 0), ("S2", 3), ("S3", 2), ("C2", 0), ("C", 1), ("C3", 0), ("C2", 1), ("S3", 3), ("D", 0), ("C", 2), ("C3", 1), ("C2", 2), ("D", 1), ("R2", 0), ("C", 3), ("C3", 2), ("C2", 3),
    ("R3", 0), ("R2", 1), ("D", 2), ("F", 0), ("C3", 3), ("R3", 1), ("D", 3), ("F", 1), ("R2", 2), ("R2", 3), ("R3", 2), ("F", 2), ("R3", 3), ("F", 3),
)

f32 = jnp.float32
bf16 = jnp.bfloat16

CORE_SWAP = [(0, 1), (1, 0), (2, 3), (3, 2)]
CHIP_SWAP = [(0, 2), (2, 0), (1, 3), (3, 1)]
TO_MIDDLE = [(0, 1), (3, 2)]
ACROSS = [(1, 2), (2, 1)]
TO_END = [(1, 0), (2, 3)]


IN_VMEM = pl.BlockSpec(memory_space=pltpu.VMEM)
IN_SMEM = pl.BlockSpec(memory_space=pltpu.SMEM)
MIB = 2**20


def call(body, place, arrays, weight, outs):
    rows = arrays[0].shape[0]
    return pl.pallas_call(
        body,
        out_shape=[jax.ShapeDtypeStruct((rows, width), dtype) for width, dtype in outs],
        in_specs=[IN_SMEM] + [IN_VMEM] * (len(arrays) + 1),
        out_specs=[IN_VMEM] * len(outs),
        compiler_params=pltpu.CompilerParams(vmem_limit_bytes=8 * MIB),
        cost_estimate=pl.CostEstimate(
            flops=2 * rows * weight.shape[0] * weight.shape[1], bytes_accessed=2 * weight.size, transcendentals=0
        ),
    )(place, *arrays, pltpu.with_memory_space_constraint(weight, pltpu.VMEM))


def columns(at, width):
    return pl.ds(pl.multiple_of(at, 128), width)


def tile_of(width):
    return next(t for t in (768, 512, 384, 256, 128) if width % t == 0)


def encode_kernel(place, x, w, sent, mine):
    half = sent.shape[1]
    tile = tile_of(half)
    for out, core in ((sent, 1 - place[0]), (mine, place[0])):

        @pl.loop(0, half // tile)
        def _(j):
            out[:, columns(j * tile, tile)] = jnp.dot(
                x[...], w[:, columns(core * half + j * tile, tile)], preferred_element_type=f32
            )


def decode_kernel(place, mine, got, w, out):
    half, width = mine.shape[1], out.shape[1]
    tile = tile_of(width)
    own_rows = columns(place[0] * half, half)
    got_rows = columns((1 - place[0]) * half, half)

    @pl.loop(0, width // tile)
    def _(j):
        at = columns(j * tile, tile)
        total = jnp.dot(mine[...], w[own_rows, at], preferred_element_type=f32)
        total += jnp.dot(got[...], w[got_rows, at], preferred_element_type=f32)
        out[:, at] = total.astype(out.dtype)


def dot_rows(x, w):
    return lax.dot_general(w, x, (((1,), (1,)), ((), ())), preferred_element_type=f32).T


def grad_kernel(place, err, got, w, sent, mine):
    half = sent.shape[1]
    tile = tile_of(half)

    def fill(x):
        for out, core in ((sent, 1 - place[0]), (mine, place[0])):

            @pl.loop(0, half // tile)
            def _(j):
                part = dot_rows(x[...], w[columns(core * half + j * tile, tile), :])
                out[:, columns(j * tile, tile)] = part.astype(out.dtype)

    at_end = (place[1] == 0) | (place[1] == 3)
    pl.when(at_end)(lambda: fill(got))
    pl.when(jnp.logical_not(at_end))(lambda: fill(err))


def input_kernel(place, mine, got, w, first, rest):
    half, quarter = mine.shape[1], first.shape[1]
    own_columns = columns(place[0] * half, half)
    got_columns = columns((1 - place[0]) * half, half)

    def dot(m):
        rows = columns(jnp.where(place[1] < 2, m, 3 - m) * quarter, quarter)
        total = dot_rows(mine[...], w[rows, own_columns]) + dot_rows(got[...], w[rows, got_columns])
        return total.astype(first.dtype)

    @pl.loop(0, 3)
    def _(m):
        rest[:, columns(m * quarter, quarter)] = dot(m + 1)

    first[...] = dot(0)


def add_pair(mine, got):
    return (mine.astype(f32) + got.astype(f32)).astype(mine.dtype)


def local(inputs, clean_acts, enc_weight, enc_bias, dec_weight, dec_bias, pairing, targets):
    row_count = inputs.shape[0]
    lat_count = enc_weight.shape[2]
    inputs, clean_acts = inputs[:, 0], clean_acts[:, 0]
    enc, dec = enc_weight[0], dec_weight[0]
    core = lax.axis_index("layer") % 2
    z = lax.axis_index("latent")
    end = (z == 0) | (z == 3)
    row_ids = lax.axis_index("row") * row_count + jnp.arange(row_count, dtype=jnp.int32)
    own_target = lax.dynamic_slice_in_dim(targets, row_ids[0], row_count)
    moved_target = jnp.sum(jnp.where(pairing[None, :] == row_ids[:, None], targets[None, :], 0), axis=1)
    half = lat_count // 2
    ids_half = (z * lat_count + core * half + jnp.arange(half, dtype=jnp.int32))[None]
    bias_half = lax.dynamic_slice_in_dim(enc_bias, core * half, half)[None]

    starts = [sum(CHUNKS[:k]) for k in range(len(CHUNKS))]
    state = [{} for _ in CHUNKS]

    def rows(array, k):
        return array[starts[k] : starts[k] + CHUNKS[k]]

    place = jnp.stack([core, z]).astype(jnp.int32)
    quarter = dec.shape[1] // 4

    def step_a(k, s):
        sent, s["mine"] = call(encode_kernel, place, [s["x"]], enc, [(half, f32), (half, f32)])
        return sent, "layer", CORE_SWAP

    def step_a2(k, s):
        s["pair"] = s["mine"] + s["got"]
        return s["pair"], "layer", CHIP_SWAP

    def step_a3(k, s):
        s["preact"] = s["pair"] + s["got"] + bias_half
        s["feat"] = jnp.maximum(s["preact"], 0.0).astype(bf16)
        return s["feat"], "layer", CORE_SWAP

    def step_b(k, s):
        (s["part"],) = call(decode_kernel, place, [s["feat"], s["got"]], dec, [(dec.shape[1], bf16)])
        return s["part"], "latent", TO_MIDDLE

    def step_s2(k, s):
        s["pair"] = add_pair(s["part"], s["got"])
        return s["pair"], "latent", ACROSS

    def step_s3(k, s):
        total = s["pair"].astype(f32) + s["got"].astype(f32)
        s["err"] = (total + dec_bias - rows(clean_acts, k).astype(f32)).astype(bf16)
        return s["err"], "latent", TO_END

    def step_c(k, s):
        sent, s["mine"] = call(grad_kernel, place, [s["err"], s["got"]], dec, [(half, bf16), (half, bf16)])
        return sent, "layer", CORE_SWAP

    def step_c2(k, s):
        s["pair"] = add_pair(s["mine"], s["got"])
        return s["pair"], "layer", CHIP_SWAP

    def step_c3(k, s):
        grad = s["pair"].astype(f32) + s["got"].astype(f32)
        margin = (rows(own_target, k)[:, None] == ids_half).astype(f32)
        margin = margin - (rows(moved_target, k)[:, None] == ids_half).astype(f32)
        s["pre"] = jnp.where(s["preact"] > 0, grad - MARGIN * margin, 0.0).astype(bf16)
        return s["pre"], "layer", CORE_SWAP

    def step_d(k, s):
        s["first"], s["rest"] = call(
            input_kernel, place, [s["pre"], s["got"]], enc, [(quarter, bf16), (3 * quarter, bf16)]
        )
        return s["rest"], "latent", TO_MIDDLE

    def step_r2(k, s):
        s["own_mid"] = add_pair(s["rest"][:, :quarter], s["got"][:, :quarter])
        s["mid"] = add_pair(s["rest"][:, quarter:], s["got"][:, quarter:])
        return s["mid"], "latent", ACROSS

    def step_r3(k, s):
        s["own_mid"] = add_pair(s["own_mid"], s["got"][:, :quarter])
        s["for_end"] = add_pair(s["first"], s["got"][:, quarter:])
        return s["for_end"], "latent", TO_END

    def step_f(k, s):
        s["done"] = jnp.where(end, add_pair(s["first"], s["got"]), s["own_mid"])
        return s["done"], None, None

    steps = {
        "A": (step_a, ("x",)),
        "A2": (step_a2, ("mine", "got")),
        "A3": (step_a3, ("pair", "got")),
        "B": (step_b, ("feat", "got")),
        "S2": (step_s2, ("part", "got")),
        "S3": (step_s3, ("pair", "got")),
        "C": (step_c, ("err", "got")),
        "C2": (step_c2, ("mine", "got")),
        "C3": (step_c3, ("pair", "got")),
        "D": (step_d, ("pre", "got")),
        "R2": (step_r2, ("rest", "got")),
        "R3": (step_r3, ("first", "own_mid", "got")),
        "F": (step_f, ("first", "own_mid", "got")),
    }
    for k, s in enumerate(state):
        s["x"] = rows(inputs, k)
    token = None
    for name, k in ORDER:
        s = state[k]
        step, names = steps[name]
        if token is not None:
            *held, _ = lax.optimization_barrier((*[s[n] for n in names], token))
            s.update(zip(names, held))
        token, axis, pairs = step(k, s)
        if axis is not None:
            s["got"] = lax.ppermute(token, axis, pairs)
    return jnp.concatenate([s["done"] for s in state], axis=0)[:, None]


def plain(inputs, clean_acts, enc_weight, enc_bias, dec_weight, dec_bias, pairing, targets):
    row_count = inputs.shape[0]
    lat_count = enc_weight.shape[2]
    partial_pre = jnp.einsum("rld,ldf->rf", inputs, enc_weight, preferred_element_type=f32)
    preact = lax.psum(partial_pre, "layer") + enc_bias
    features = jnp.maximum(preact, 0.0).astype(bf16)
    part = jnp.einsum("rf,lfd->rld", features, dec_weight, preferred_element_type=f32)
    recon = lax.psum(part.astype(bf16), "latent").astype(f32) + dec_bias[None]
    err = (recon - clean_acts.astype(f32)).astype(bf16)
    grad = jnp.einsum("rld,lfd->rf", err, dec_weight, preferred_element_type=f32)
    grad = lax.psum(grad.astype(bf16), "layer").astype(f32)
    row_ids = lax.axis_index("row") * row_count + jnp.arange(row_count, dtype=jnp.int32)
    ids = lax.axis_index("latent") * lat_count + jnp.arange(lat_count, dtype=jnp.int32)
    own_target = lax.dynamic_slice_in_dim(targets, row_ids[0], row_count)[:, None]
    moved_target = jnp.sum(jnp.where(pairing[None, :] == row_ids[:, None], targets[None, :], 0), axis=1)[:, None]
    margin = (own_target == ids).astype(f32) - (moved_target == ids).astype(f32)
    pre = jnp.where(preact > 0, grad - MARGIN * margin, 0.0).astype(bf16)
    out = jnp.einsum("rf,ldf->rld", pre, enc_weight, preferred_element_type=f32)
    return lax.psum_scatter(out.astype(bf16), "latent", scatter_dimension=2, tiled=True)


def solution(mesh):
    placed = (
        P("row", "layer", None),
        P("row", "layer", None),
        P("layer", None, "latent"),
        P("latent"),
        P("layer", "latent", None),
        P("layer", None),
        P(),
        P(),
    )
    line = mesh.shape["latent"] == 4 and mesh.shape["layer"] == 4
    return jax.shard_map(
        local if line else plain,
        mesh=mesh,
        in_specs=placed,
        out_specs=P("row", "layer", "latent"),
        check_vma=False,
    )
```

```python
import jax
import jax.numpy as jnp
from jax import lax
from jax.experimental import pallas as pl
from jax.experimental.pallas import tpu as pltpu
from jax.sharding import PartitionSpec as P

MARGIN = 16.0
CHUNKS = (128, 128, 128, 128)
ORDER = (
    ("A", (0,)), ("A", (2,)), ("A2", (0,)), ("A", (1,)), ("A2", (2,)), ("A", (3,)), ("A3", (0,)), ("A2", (1,)),
    ("B", (0,)), ("A3", (2,)), ("A2", (3,)), ("B", (2,)), ("A3", (1,)), ("S2", (0,)), ("B", (1,)), ("A3", (3,)),
    ("S2", (2,)), ("S3", (0,)), ("B", (3,)), ("S2", (1,)), ("S3", (2,)), ("C", (0,)), ("S2", (3,)), ("C2", (0,)),
    ("S3", (1,)), ("C", (2,)), ("C3", (0,)), ("S3", (3,)), ("D", (0,)), ("C", (1,)), ("C2", (2,)), ("C", (3,)),
    ("R2", (0,)), ("C3", (2,)), ("C2", (3,)), ("C2", (1,)), ("D", (2,)), ("C3", (3,)), ("C3", (1,)), ("D", (3,)),
    ("R2", (2,)), ("D", (1,)), ("R2", (3,)), ("R3", (2,)), ("R3", (0,)), ("F", (2,)), ("R3", (3,)), ("R2", (1,)),
    ("F", (0,)), ("F", (3,)), ("R3", (1,)), ("F", (1,)),
)

f32 = jnp.float32
bf16 = jnp.bfloat16

CORE_SWAP = [(0, 1), (1, 0), (2, 3), (3, 2)]
CHIP_SWAP = [(0, 2), (2, 0), (1, 3), (3, 1)]
TO_MIDDLE = [(0, 1), (3, 2)]
ACROSS = [(1, 2), (2, 1)]
TO_END = [(1, 0), (2, 3)]


IN_VMEM = pl.BlockSpec(memory_space=pltpu.VMEM)
IN_HBM = pl.BlockSpec(memory_space=pl.ANY)
IN_SMEM = pl.BlockSpec(memory_space=pltpu.SMEM)
MIB = 2**20


def call(body, place, arrays, outs, scratch=(), limit=8):
    return pl.pallas_call(
        body,
        out_shape=[jax.ShapeDtypeStruct(*out) for out in outs],
        in_specs=[IN_SMEM] + [IN_HBM if space == pltpu.HBM else IN_VMEM for _, space in arrays],
        out_specs=[IN_VMEM] * len(outs),
        scratch_shapes=scratch,
        compiler_params=pltpu.CompilerParams(vmem_limit_bytes=limit * MIB),
        cost_estimate=pl.CostEstimate(flops=1, bytes_accessed=1, transcendentals=0),
    )(place, *[a if space is None else pltpu.with_memory_space_constraint(a, space) for a, space in arrays])


def span(at, width):
    return pl.ds(pl.multiple_of(at, 128), width)


def tile_of(width, most):
    return next(t for t in range(most - most % 128, 0, -128) if width % t == 0)


def fetch(w, held, sems, tiles, part):
    @pl.loop(0, tiles)
    def _(j):
        pltpu.make_async_copy(w.at[part(j)], held.at[part(j)], sems.at[j]).start()


def wait(w, held, sems, part, j):
    pltpu.make_async_copy(w.at[part(j)], held.at[part(j)], sems.at[j]).wait()


def fetched(w, tiles):
    return [pltpu.VMEM(w.shape, w.dtype), pltpu.SemaphoreType.DMA((tiles,))]


def encode(place, x, w, at, sizes):
    half = w.shape[1] // 2
    tile = tile_of(half, 512)
    n = half // tile
    count = sum(sizes)

    def body(p, x, w, *refs):
        outs, (held, sems, rows, sem) = refs[: 2 * len(sizes)], refs[2 * len(sizes) :]
        copy = pltpu.make_async_copy(x.at[pl.ds(at, count)], rows, sem)
        copy.start()
        part = lambda j: (slice(None), span((j + (1 - p[0]) * n) % (2 * n) * tile, tile))
        fetch(w, held, sems, 2 * n, part)
        copy.wait()
        for side, first in ((0, 0), (1, n)):

            @pl.loop(0, n)
            def _(j):
                wait(w, held, sems, part, first + j)
                got = jnp.dot(rows[...], held[part(first + j)], preferred_element_type=f32)
                start = 0
                for out, size in zip(outs[side :: 2], sizes):
                    out[:, span(j * tile, tile)] = got[start : start + size]
                    start += size

    scratch = fetched(w, 2 * n) + [pltpu.VMEM((count, x.shape[1]), x.dtype), pltpu.SemaphoreType.DMA]
    outs = [((size, half), f32) for size in sizes for _ in range(2)]
    return call(body, place, [(x, pltpu.HBM), (w, pltpu.HBM)], outs, scratch, 24 + count // 32)


def gather_halves(p, pairs, x):
    start, half = 0, x.shape[1] // 2
    for mine, got in pairs:
        rows = pl.ds(start, mine.shape[0])
        x[rows, span(p[0] * half, half)] = mine[...]
        x[rows, span((1 - p[0]) * half, half)] = got[...]
        start += mine.shape[0]


def spread(outs, at, value):
    start = 0
    for out in outs:
        out[:, at] = value[start : start + out.shape[0]]
        start += out.shape[0]


def pairs_of(refs):
    return list(zip(refs[::2], refs[1::2]))


def decode(place, chunks, w):
    width = w.shape[1]
    tile = tile_of(width, 512)
    n = width // tile
    k = len(chunks)
    sizes = [mine.shape[0] for mine, _ in chunks]

    def body(p, *refs):
        pairs, w, outs, (held, sems, x) = pairs_of(refs[: 2 * k]), refs[2 * k], refs[2 * k + 1 : -3], refs[-3:]
        part = lambda j: (slice(None), span(j * tile, tile))
        fetch(w, held, sems, n, part)
        gather_halves(p, pairs, x)

        @pl.loop(0, n)
        def _(j):
            wait(w, held, sems, part, j)
            total = jnp.dot(x[...], held[part(j)], preferred_element_type=f32)
            spread(outs, span(j * tile, tile), total.astype(bf16))

    arrays = [(a, None) for pair in chunks for a in pair] + [(w, pltpu.HBM)]
    scratch = [*fetched(w, n), pltpu.VMEM((sum(sizes), w.shape[0]), bf16)]
    return call(body, place, arrays, [((size, width), bf16) for size in sizes], scratch, 28 + sum(sizes) // 32)


def dot_rows(x, w):
    return lax.dot_general(w, x, (((1,), (1,)), ((), ())), preferred_element_type=f32)


def gradient(place, chunks, w):
    half = w.shape[0] // 2
    tile = tile_of(half, 512)
    n = half // tile
    k = len(chunks)
    sizes = [err.shape[0] for err, _ in chunks]

    def body(p, *refs):
        pairs, w, outs, (held, sems, x) = pairs_of(refs[: 2 * k]), refs[2 * k], refs[2 * k + 1 : -3], refs[-3:]
        part = lambda j: (span((j + (1 - p[0]) * n) % (2 * n) * tile, tile), slice(None))
        fetch(w, held, sems, 2 * n, part)
        at_end = (p[1] == 0) | (p[1] == 3)
        start = 0
        for err, got in pairs:
            x[pl.ds(start, err.shape[0]), :] = jnp.where(at_end, got[...], err[...])
            start += err.shape[0]
        for side, first in ((0, 0), (1, n)):

            @pl.loop(0, n)
            def _(j):
                wait(w, held, sems, part, first + j)
                total = dot_rows(x[...], held[part(first + j)])
                spread(outs[side::2], span(j * tile, tile), total.T.astype(bf16))

    arrays = [(a, None) for pair in chunks for a in pair] + [(w, pltpu.HBM)]
    outs = [((size, half), bf16) for size in sizes for _ in range(2)]
    scratch = [*fetched(w, 2 * n), pltpu.VMEM((sum(sizes), w.shape[1]), bf16)]
    return call(body, place, arrays, outs, scratch, 28 + sum(sizes) // 32)


def input_part(place, chunks, w):
    quarter = w.shape[0] // 4
    k = len(chunks)
    sizes = [mine.shape[0] for mine, _ in chunks]

    def body(p, *refs):
        pairs, w, outs, (held, sems, x) = pairs_of(refs[: 2 * k]), refs[2 * k], refs[2 * k + 1 : -3], refs[-3:]
        part = lambda j: (span(jnp.where(p[1] < 2, (j + 1) % 4, (6 - j) % 4) * quarter, quarter), slice(None))
        fetch(w, held, sems, 4, part)
        gather_halves(p, pairs, x)

        def dot(j):
            wait(w, held, sems, part, j)
            return dot_rows(x[...], held[part(j)]).T.astype(bf16)

        @pl.loop(0, 3)
        def _(j):
            spread(outs[::2], span(j * quarter, quarter), dot(j))

        spread(outs[1::2], slice(None), dot(3))

    arrays = [(a, None) for pair in chunks for a in pair] + [(w, pltpu.HBM)]
    outs = [((size, count * quarter), bf16) for size in sizes for count in (3, 1)]
    scratch = [*fetched(w, 4), pltpu.VMEM((sum(sizes), w.shape[1]), bf16)]
    return call(body, place, arrays, outs, scratch, 28 + sum(sizes) // 32)


def add_pair(mine, got):
    return (mine.astype(f32) + got.astype(f32)).astype(mine.dtype)


def local(inputs, clean_acts, enc_weight, enc_bias, dec_weight, dec_bias, pairing, targets):
    row_count = inputs.shape[0]
    lat_count = enc_weight.shape[2]
    inputs, clean_acts = inputs[:, 0], clean_acts[:, 0]
    enc, dec = enc_weight[0], dec_weight[0]
    core = lax.axis_index("layer") % 2
    z = lax.axis_index("latent")
    end = (z == 0) | (z == 3)
    row_ids = lax.axis_index("row") * row_count + jnp.arange(row_count, dtype=jnp.int32)
    own_target = lax.dynamic_slice_in_dim(targets, row_ids[0], row_count)
    moved_target = jnp.sum(jnp.where(pairing[None, :] == row_ids[:, None], targets[None, :], 0), axis=1)
    half = lat_count // 2
    ids_half = (z * lat_count + core * half + jnp.arange(half, dtype=jnp.int32))[None]
    bias_half = lax.dynamic_slice_in_dim(enc_bias, core * half, half)[None]

    starts = [sum(CHUNKS[:k]) for k in range(len(CHUNKS))]
    state = [{} for _ in CHUNKS]

    def rows(array, k):
        return array[starts[k] : starts[k] + CHUNKS[k]]

    place = jnp.stack([core, z]).astype(jnp.int32)
    quarter = dec.shape[1] // 4

    def step_a2(k, s):
        s["pair"] = s["mine"] + s["got"]
        return s["pair"], "layer", CHIP_SWAP

    def step_a3(k, s):
        s["preact"] = s["pair"] + s["got"] + bias_half
        s["feat"] = jnp.maximum(s["preact"], 0.0).astype(bf16)
        return s["feat"], "layer", CORE_SWAP

    def step_s2(k, s):
        s["pair"] = add_pair(s["part"], s["got"])
        return s["pair"], "latent", ACROSS

    def step_s3(k, s):
        total = s["pair"].astype(f32) + s["got"].astype(f32)
        s["err"] = (total + dec_bias - rows(clean_acts, k).astype(f32)).astype(bf16)
        return s["err"], "latent", TO_END

    def step_c2(k, s):
        s["pair"] = add_pair(s["mine"], s["got"])
        return s["pair"], "layer", CHIP_SWAP

    def step_c3(k, s):
        grad = s["pair"].astype(f32) + s["got"].astype(f32)
        margin = (rows(own_target, k)[:, None] == ids_half).astype(f32)
        margin = margin - (rows(moved_target, k)[:, None] == ids_half).astype(f32)
        s["pre"] = jnp.where(s["preact"] > 0, grad - MARGIN * margin, 0.0).astype(bf16)
        return s["pre"], "layer", CORE_SWAP

    def step_r2(k, s):
        s["own_mid"] = add_pair(s["rest"][:, :quarter], s["got"][:, :quarter])
        s["mid"] = add_pair(s["rest"][:, quarter:], s["got"][:, quarter:])
        return s["mid"], "latent", ACROSS

    def step_r3(k, s):
        s["own_mid"] = add_pair(s["own_mid"], s["got"][:, :quarter])
        s["for_end"] = add_pair(s["first"], s["got"][:, quarter:])
        return s["for_end"], "latent", TO_END

    def step_f(k, s):
        s["done"] = jnp.where(end, add_pair(s["first"], s["got"]), s["own_mid"])
        return s["done"], None, None

    steps = {
        "A2": (step_a2, ("mine", "got")),
        "A3": (step_a3, ("pair", "got")),
        "S2": (step_s2, ("part", "got")),
        "S3": (step_s3, ("pair", "got")),
        "C2": (step_c2, ("mine", "got")),
        "C3": (step_c3, ("pair", "got")),
        "R2": (step_r2, ("rest", "got")),
        "R3": (step_r3, ("first", "own_mid", "got")),
        "F": (step_f, ("first", "own_mid", "got")),
    }
    matmuls = {
        "B": (decode, dec, ("feat", "got"), ("part",), "latent", TO_MIDDLE),
        "C": (gradient, dec, ("err", "got"), ("sent", "mine"), "layer", CORE_SWAP),
        "D": (input_part, enc, ("pre", "got"), ("rest", "first"), "latent", TO_MIDDLE),
    }

    token = None
    for name, ks in ORDER:
        if name == "A":
            held = place if token is None else lax.optimization_barrier((place, token))[0]
            results = encode(held, inputs, enc, starts[ks[0]], [CHUNKS[k] for k in ks])
            given, axis, pairs = ("sent", "mine"), "layer", CORE_SWAP
        elif name in matmuls:
            kernel, weight, names, given, axis, pairs = matmuls[name]
            *held, _ = lax.optimization_barrier((*[state[k][n] for k in ks for n in names], token))
            results = kernel(place, list(zip(held[::2], held[1::2])), weight)
        else:
            (k,) = ks
            s = state[k]
            step, names = steps[name]
            *held, _ = lax.optimization_barrier((*[s[n] for n in names], token))
            s.update(zip(names, held))
            token, axis, pairs = step(k, s)
            results, given = [token], ("sent",)
        token = results[0]
        for i, k in enumerate(ks):
            state[k].update(zip(given, results[i * len(given) :]))
            if axis is not None:
                state[k]["got"] = lax.ppermute(state[k][given[0]], axis, pairs)
    return jnp.concatenate([s["done"] for s in state], axis=0)[:, None]


def plain(inputs, clean_acts, enc_weight, enc_bias, dec_weight, dec_bias, pairing, targets):
    row_count = inputs.shape[0]
    lat_count = enc_weight.shape[2]
    partial_pre = jnp.einsum("rld,ldf->rf", inputs, enc_weight, preferred_element_type=f32)
    preact = lax.psum(partial_pre, "layer") + enc_bias
    features = jnp.maximum(preact, 0.0).astype(bf16)
    part = jnp.einsum("rf,lfd->rld", features, dec_weight, preferred_element_type=f32)
    recon = lax.psum(part.astype(bf16), "latent").astype(f32) + dec_bias[None]
    err = (recon - clean_acts.astype(f32)).astype(bf16)
    grad = jnp.einsum("rld,lfd->rf", err, dec_weight, preferred_element_type=f32)
    grad = lax.psum(grad.astype(bf16), "layer").astype(f32)
    row_ids = lax.axis_index("row") * row_count + jnp.arange(row_count, dtype=jnp.int32)
    ids = lax.axis_index("latent") * lat_count + jnp.arange(lat_count, dtype=jnp.int32)
    own_target = lax.dynamic_slice_in_dim(targets, row_ids[0], row_count)[:, None]
    moved_target = jnp.sum(jnp.where(pairing[None, :] == row_ids[:, None], targets[None, :], 0), axis=1)[:, None]
    margin = (own_target == ids).astype(f32) - (moved_target == ids).astype(f32)
    pre = jnp.where(preact > 0, grad - MARGIN * margin, 0.0).astype(bf16)
    out = jnp.einsum("rf,ldf->rld", pre, enc_weight, preferred_element_type=f32)
    return lax.psum_scatter(out.astype(bf16), "latent", scatter_dimension=2, tiled=True)


def solution(mesh):
    placed = (
        P("row", "layer", None),
        P("row", "layer", None),
        P("layer", None, "latent"),
        P("latent"),
        P("layer", "latent", None),
        P("layer", None),
        P(),
        P(),
    )
    line = mesh.shape["latent"] == 4 and mesh.shape["layer"] == 4
    return jax.shard_map(
        local if line else plain,
        mesh=mesh,
        in_specs=placed,
        out_specs=P("row", "layer", "latent"),
        check_vma=False,
    )
```
